32 devices in a mesh: expert: 16 (over z, y, x), dp: 2 (over core).
Axes of the slice: x: 2, y: 2, z: 4, core: 2. Of those that a mesh axis runs over, the one named last changes fastest.
Arguments:
- tokens: bfloat16 [4096, 2048], P(('expert', 'dp')), may hold values from -6 to 6
- out_grad: bfloat16 [4096, 2048], P(('expert', 'dp')), may hold values from -6 to 6
- gates: float32 [4096, 8], P(('expert', 'dp')), may hold values from 0.05 to 0.5
- expert_ids: int32 [4096, 8], P(('expert', 'dp')), may hold values from 0 to 15, all different within a row; in each aligned block of 128 rows (0 to 127, 128 to 255, ...) at most 80 rows name the same one
- w_gate: bfloat16 [16, 2048, 384], P('expert', 'dp'), may hold values from -0.125 to 0.125
- w_up: bfloat16 [16, 2048, 384], P('expert', 'dp'), may hold values from -0.125 to 0.125
- w_down: bfloat16 [16, 2048, 384], P('expert', 'dp'), may hold values from -0.3125 to 0.3125
Outputs:
- input_grad: bfloat16 [4096, 2048], P(('expert', 'dp'))
- grad_gate: float32 [16, 2048, 384], P('expert', 'dp')
- grad_up: float32 [16, 2048, 384], P('expert', 'dp')
- grad_down: float32 [16, 2048, 384], P('expert', 'dp')
The draws below stay inside these ranges and needn't reach their ends.
Inputs may be any that keep to these rules, and one draw needn't show every extreme that they name: `expert_ids`: among the 128 tokens of one device no expert is named more than 80 times, and in every draw some device names some expert exactly 80 times. The ids of one token differ.
All inputs are finite; a program needn't handle non-finite values.
Results may differ from the reference program's by a relative error of at most 0.0065.
Values may be sent and summed in bfloat16 or wider, within the bound.
No kernel may reach another device: no remote copies, remote signals or barrier semaphores. Data moves between devices by JAX's collectives and lax.ppermute only.
A program may use at most 128 MiB of HBM per device.

```python
import math
import jax
import jax.numpy as jnp
import numpy as np
from jax import lax

D = 2048
FF = 384
TOP = 8
TOK_DEV = 128
EXPERTS = 16
CAP = 80
TOKENS = 4096
N_EXPERT = 16
N_DP = 2


def block_levels(key, shape, pieces, smallest, top_value):
    def one(axis_at, parts):
        heights = jax.random.uniform(jax.random.fold_in(jax.random.fold_in(key, 6), axis_at), (parts,), jnp.float32, smallest / len(pieces), top_value / len(pieces))
        return jnp.repeat(jnp.exp(heights), shape[axis_at] // parts).reshape((-1,) + (1,) * (len(shape) - axis_at - 1))

    level = one(*pieces[0])
    for cut in pieces[1:]:
        level = level * one(*cut)
    return level


def deal_out(own_key, own, number, rows, number_of, top, most, lean):
    ranking = jax.random.permutation(own_key, number_of)
    heavy_load, ordinary = shares(number_of, rows * top, most, lean, True), shares(number_of, rows * top, most, lean, False)
    places = jnp.arange(number_of)

    def named(sizes, rotation):
        used = int((sizes > 0).sum())
        fixed = max(1, used // 4)
        moved = fixed + (places - fixed + rotation * (used - fixed)) % max(1, number_of - fixed)
        return jnp.zeros((number_of,), jnp.int32).at[ranking[jnp.where(places < fixed, places, moved)]].set(jnp.asarray(sizes, jnp.int32))

    sizes = jnp.where(number % 4 == 0, named(heavy_load, number // 4), named(ordinary, number - number // 4 - 1))
    mixed = jax.random.permutation(jax.random.fold_in(own, 3), number_of)
    donor, receiver = mixed[0:number_of // 2 * 2:2], mixed[1:number_of // 2 * 2:2]
    slack = jnp.minimum(sizes[donor] - 1, most - sizes[receiver]) // 2
    slack = jnp.where((donor == ranking[0]) | (receiver == ranking[0]) | (sizes[receiver] == 0), 0, jnp.maximum(slack, 0))
    moved = jax.random.randint(jax.random.fold_in(own, 4), (number_of // 2,), 0, 1 << 20) % (slack + 1)
    sizes = sizes.at[donor].add(-moved).at[receiver].add(moved)
    members = jnp.searchsorted(jnp.cumsum(sizes), jnp.arange(rows * top), side="right").astype(jnp.int32)
    table = members.reshape(top, rows).T
    table = table[jax.random.permutation(jax.random.fold_in(own, 1), rows)]
    rotation = jax.random.randint(jax.random.fold_in(own, 2), (rows, 1), 0, top)
    return jnp.take_along_axis(table, (jnp.arange(top)[None, :] + rotation) % top, axis=1)


def shares(amount, total, bound, lean, full):
    weights = [(1 << 20) // math.isqrt(rank ** lean) + 1 for rank in range(1, amount + 1)]
    largest = bound if full else min(bound, max(-(-total // amount), total * weights[0] // sum(weights)))
    least = 1 if total - largest >= amount - 1 else 0
    holding, spare = [largest] + [least] * (amount - 1), total - largest - least * (amount - 1)
    while spare > 0:
        candidates = [i for i in range(1, amount) if holding[i] < largest] or [i for i in range(1, amount) if holding[i] < bound]
        pool, left = sum([weights[i] for i in candidates]), spare
        for i in candidates:
            addition = min(bound - holding[i], max(1, left * weights[i] // pool), spare)
            holding[i] = holding[i] + addition
            spare = spare - addition
    return np.array(holding)


def scatter_about(rng, dims, deviation, bound, pieces=(), kind=jnp.bfloat16):
    result = jax.random.normal(rng, dims, jnp.float32) * deviation
    if len(pieces) > 0:
        result = block_levels(rng, dims, pieces, -0.22, 0.18) * result
    return jnp.clip(result, min=-bound, max=bound).astype(kind)


def setup_inputs(seed: int = 0) -> dict:
    splits = jax.random.split(jax.random.key(seed), 8)
    tokens = scatter_about(splits[0], (TOKENS, D), 1.0, 6.0, ((0, 32),))
    out_grad = scatter_about(splits[1], (TOKENS, D), 1.0, 6.0, ((0, 32),))
    gates = jnp.clip(jnp.exp(math.log(0.5) - 2.3025851 * jax.random.uniform(splits[2], (TOKENS, TOP), jnp.float32) ** block_levels(splits[2], (TOKENS, TOP), ((0, 32),), -0.2, 0.2)), 0.05, 0.5)
    expert_ids_keys = jax.random.split(jax.random.fold_in(splits[3], 1), TOKENS // TOK_DEV)
    expert_ids_turns = jax.random.permutation(jax.random.fold_in(splits[3], 3), TOKENS // TOK_DEV)
    expert_ids = jax.vmap(lambda own, number: deal_out(jax.random.fold_in(splits[3], 2), own, number, TOK_DEV, EXPERTS, TOP, CAP, 2))(expert_ids_keys, expert_ids_turns).reshape((TOKENS, TOP))
    w_gate = scatter_about(splits[4], (EXPERTS, D, FF), D ** -0.5, 0.125, ((0, 16), (1, 2)))
    w_up = scatter_about(splits[5], (EXPERTS, D, FF), D ** -0.5, 0.125, ((0, 16), (1, 2)))
    w_down = scatter_about(splits[6], (EXPERTS, D, FF), FF ** -0.5, 0.3125, ((0, 16), (1, 2)))
    return dict(tokens=tokens, out_grad=out_grad, gates=gates, expert_ids=expert_ids, w_gate=w_gate, w_up=w_up, w_down=w_down)


def reference(tokens, out_grad, gates, expert_ids, w_gate, w_up, w_down):
    pair_count = TOKENS * TOP
    most_rows = N_EXPERT * N_DP * CAP
    flat_ids = expert_ids.reshape(-1)
    tokens_pad = jnp.concatenate([tokens, jnp.zeros((1, D), tokens.dtype)], axis=0)
    grads_pad = jnp.concatenate([out_grad, jnp.zeros((1, D), out_grad.dtype)], axis=0)
    gates_flat = jnp.concatenate([gates.reshape(-1), jnp.zeros((1,), gates.dtype)], axis=0)

    def one_expert(dx_total, inputs):
        expert, gate_w, up_w, down_w = inputs
        picked = jnp.nonzero(flat_ids == expert, size=most_rows, fill_value=pair_count)[0].astype(jnp.int32)
        tok_index = jnp.where(picked < pair_count, picked // TOP, TOKENS).astype(jnp.int32)
        x_rows = tokens_pad[tok_index]
        dy_rows = (gates_flat[picked][:, None] * grads_pad[tok_index].astype(jnp.float32)).astype(jnp.bfloat16)
        gate_pre = jnp.dot(x_rows, gate_w, preferred_element_type=jnp.float32)
        up_pre = jnp.dot(x_rows, up_w, preferred_element_type=jnp.float32)
        sig_gate = jax.nn.sigmoid(gate_pre)
        active = gate_pre * sig_gate
        hidden = (active * up_pre).astype(jnp.bfloat16)
        hidden_grad = jnp.dot(dy_rows, down_w, preferred_element_type=jnp.float32)
        gate_grad = (hidden_grad * up_pre * sig_gate * (1.0 + gate_pre * (1.0 - sig_gate))).astype(jnp.bfloat16)
        up_grad = (hidden_grad * active).astype(jnp.bfloat16)
        grad_g = jnp.dot(x_rows.T, gate_grad, preferred_element_type=jnp.float32)
        grad_u = jnp.dot(x_rows.T, up_grad, preferred_element_type=jnp.float32)
        grad_d = jnp.dot(dy_rows.T, hidden, preferred_element_type=jnp.float32)
        pair_grad = (jnp.dot(gate_grad, gate_w.T, preferred_element_type=jnp.float32)
                     + jnp.dot(up_grad, up_w.T, preferred_element_type=jnp.float32)).astype(jnp.bfloat16)
        dx_total = dx_total.at[tok_index].add(pair_grad.astype(jnp.float32))
        return dx_total, (grad_g, grad_u, grad_d)

    start_total = jnp.zeros((TOKENS + 1, D), jnp.float32)
    expert_list = jnp.arange(EXPERTS, dtype=jnp.int32)
    dx_total, grads = lax.scan(one_expert, start_total, (expert_list, w_gate, w_up, w_down))
    input_grad = dx_total[:TOKENS].astype(jnp.bfloat16)
    return input_grad, grads[0], grads[1], grads[2]
```

```python
import jax
import jax.numpy as jnp
from jax import lax
from jax.experimental import pallas as pl
from jax.experimental.pallas import tpu as pltpu
from jax.sharding import PartitionSpec as P

contract_rows = (((0,), (0,)), ((), ()))
contract_cols = (((1,), (1,)), ((), ()))
ACROSS_X, ACROSS_Y, PAIR, ACROSS_Z = 1, 2, 4, 8
low, wide = jnp.bfloat16, jnp.float32


def after(rows, *earlier):
    return lax.optimization_barrier((rows,) + earlier)[0]


def swap(rows, bit):
    if bit == 0:
        return lax.ppermute(rows, "dp", [(0, 1), (1, 0)])
    experts = lax.axis_size("expert")
    return lax.ppermute(rows, "expert", [(i, i ^ bit) for i in range(experts)])


def turn(rows):
    half = rows.shape[1] // 2
    turned = jnp.concatenate([rows[:, half:], rows[:, :half]], axis=1)
    return jnp.where(lax.axis_index("dp") == 0, rows, turned)


def gate_rows(gates, expert_ids, experts):
    count = gates.shape[0]
    lanes = lax.broadcasted_iota(jnp.int32, (1, experts * count), 1) // count
    ids = jnp.tile(expert_ids.T, (1, experts))
    spread = jnp.sum(jnp.where(ids == lanes, jnp.tile(gates.T, (1, experts)), 0.0), axis=0, keepdims=True)
    first = lax.reduce_precision(spread, 8, 7)
    second = lax.reduce_precision(spread - first, 8, 7)
    third = spread - first - second
    empty = jnp.zeros((5, experts * count), wide)
    return jnp.concatenate([first, second, third, empty], axis=0).astype(low)


def scale_of(block, rows, expert):
    terms = lax.dynamic_slice(block, (rows, expert * rows), (8, rows))
    return jnp.sum(terms.astype(wide), axis=0)


def activations(pre, out_pre, scale):
    ff = out_pre.shape[1]
    gate_pre, up_pre = pre[:, :ff], pre[:, ff:]
    hidden_grad = scale * out_pre
    sig_gate = jax.nn.sigmoid(gate_pre)
    active = gate_pre * sig_gate
    hidden = (scale * (active * up_pre)).astype(low)
    gate_grad = (hidden_grad * up_pre * sig_gate * (1.0 + gate_pre * (1.0 - sig_gate))).astype(low)
    up_grad = (hidden_grad * active).astype(low)
    return hidden, jnp.concatenate([gate_grad, up_grad], axis=1)


def dot(a, b, dims=(((1,), (0,)), ((), ()))):
    return lax.dot_general(a, b, dims, preferred_element_type=wide)


def plane_sends(dx):
    quarter = dx.shape[0] // 4
    half = quarter // 2
    own, of_x, of_y, of_xy = [dx[i * quarter : (i + 1) * quarter] for i in range(4)]
    to_y = jnp.concatenate([of_y[:half], of_xy[:half]], axis=0)
    to_x = jnp.concatenate([of_x[half:], of_xy[half:]], axis=0)
    return to_x, to_y, of_x[:half], of_y[half:], own


def plus(a, b):
    return (a.astype(wide) + b.astype(wide)).astype(low)


def plane_total(own, got_x, got_y, got_first, got_second):
    half = got_first.shape[0]
    got = (
        jnp.concatenate([got_y[:half], got_x[:half]], axis=0).astype(wide)
        + jnp.concatenate([got_first, got_second], axis=0).astype(wide)
    )
    return own.astype(wide) + got


def dx_kernel(act_a, act_b, w_a, w_b, out):
    out[...] = (dot(act_a[...], w_a[...], contract_cols) + dot(act_b[...], w_b[...], contract_cols)).astype(low)


def dx_rows(act_a, act_b, w_a, w_b):
    rows, depth = act_a.shape
    width = w_a.shape[0]
    tile = min(width, 512)
    whole = pl.BlockSpec((rows, depth), lambda i: (0, 0))
    part = pl.BlockSpec((tile, depth), lambda i: (i, 0))
    return pl.pallas_call(
        dx_kernel,
        grid=(width // tile,),
        in_specs=[whole, whole, part, part],
        out_specs=pl.BlockSpec((rows, tile), lambda i: (0, i)),
        out_shape=jax.ShapeDtypeStruct((rows, width), low),
        compiler_params=pltpu.CompilerParams(vmem_limit_bytes=24 << 20),
        cost_estimate=pl.CostEstimate(
            flops=4 * rows * depth * width, bytes_accessed=4 * width * depth + 2 * rows * width, transcendentals=0
        ),
    )(act_a, act_b, w_a, w_b)


def dense_local(tokens, out_grad, gates, expert_ids, w_gate, w_up, w_down):
    experts = lax.axis_size("expert")
    tok_rows, width = tokens.shape
    mid = width // 2
    ff = w_gate.shape[2]
    me = lax.axis_index("expert")
    pair = me ^ PAIR

    def join(parts):
        return jnp.concatenate([p[:tok_rows] for p in parts], axis=0)

    def scales(parts, expert):
        return jnp.concatenate([scale_of(p, tok_rows, expert) for p in parts])[:, None]

    def weight_sum(rows, acts, columns):
        return sum(dot(r[:, columns], a, contract_rows) for r, a in zip(rows, acts))

    keep, send = slice(0, mid), slice(mid, width)

    x_own = turn(tokens)
    g_own = jnp.concatenate([turn(out_grad), gate_rows(gates, expert_ids, experts)], axis=0)
    both_mine = jnp.concatenate([w_gate[0], w_up[0]], axis=1)
    down_mine = w_down[0]
    both_pair = swap(both_mine, PAIR)
    x_far = swap(x_own, ACROSS_Z)
    x_x = swap(x_own, ACROSS_X)
    g_y = swap(g_own, ACROSS_Y)
    both_other = swap(both_mine, 0)
    down_other = swap(after(down_mine, both_other), 0)
    g_far = swap(after(g_own, both_other), ACROSS_Z)
    g_x = swap(after(g_own, x_x, g_y, both_other), ACROSS_X)
    x_y = swap(after(x_own, x_x, g_y, both_other), ACROSS_Y)
    g_y, x_x = after((g_y, x_x), g_x, x_y, down_other)
    g_xy = swap(g_y, ACROSS_X)
    x_xy = swap(x_x, ACROSS_Y)
    x_far = after(x_far, g_xy, x_xy)
    x_far_x = swap(x_far, ACROSS_X)
    x_far_y = swap(x_far, ACROSS_Y)
    down_pair = swap(after(down_mine, x_far), PAIR)
    both_pair = after(both_pair, x_far)
    both_pair_other = swap(both_pair, 0)
    both_a = jnp.concatenate([both_mine, both_other], axis=0)
    down_a = jnp.concatenate([down_mine, down_other], axis=0)
    x_near_parts = after((x_own, x_x, x_y, x_xy), x_far)
    g_near_parts = after((g_own, g_x, g_y, g_xy), x_far)
    x_near, g_near = join(x_near_parts), join(g_near_parts)
    hid_a_near, act_a_near = activations(
        dot(x_near, both_a), dot(g_near, down_a), scales(g_near_parts, me)
    )
    g_far = after(g_far, x_far_x, x_far_y, act_a_near)
    g_far_x = swap(g_far, ACROSS_X)
    g_far_y = swap(g_far, ACROSS_Y)
    both_b = jnp.concatenate([both_pair, both_pair_other], axis=0)
    x_near, g_near, both_b = after((x_near, g_near, both_b), g_far)
    pre_b_near = dot(x_near, both_b)
    near_a = [
        dot(r[:, c], v, contract_rows)
        for r, v in ((x_near, act_a_near), (g_near, hid_a_near))
        for c in (send, keep)
    ]
    g_far_y, x_far_x = after((g_far_y, x_far_x), g_far_x, pre_b_near, *near_a)
    g_far_xy = swap(g_far_y, ACROSS_X)
    x_far_xy = swap(x_far_x, ACROSS_Y)
    down_pair = after(down_pair, g_far_y)
    down_b = jnp.concatenate([down_pair, swap(down_pair, 0)], axis=0)
    hid_b_near, act_b_near = activations(pre_b_near, dot(g_near, down_b), scales(g_near_parts, pair))
    g_far_xy, x_far_xy = after((g_far_xy, x_far_xy), act_b_near)
    x_far_parts = (x_far, x_far_x, x_far_y, x_far_xy)
    g_far_parts = (g_far, g_far_x, g_far_y, g_far_xy)
    x_fars, g_fars = join(x_far_parts), join(g_far_parts)
    hid_b_far, act_b_far = activations(
        dot(x_fars, both_b), dot(g_fars, down_b), scales(g_far_parts, pair)
    )
    pairs_b = ((x_near, x_fars), (act_b_near, act_b_far)), ((g_near, g_fars), (hid_b_near, hid_b_far))
    sent = [weight_sum(r, v, send).astype(low) for r, v in pairs_b]
    got = [swap(sent[0], 0)]
    got.append(swap(after(sent[1], got[0]), 0))
    kept = [weight_sum(r, v, keep) for r, v in pairs_b]
    for_pair = [(k + g.astype(wide)).astype(low) for k, g in zip(kept, got)]
    from_pair = [swap(for_pair[0], PAIR), swap(for_pair[1], PAIR)]
    x_fars, g_fars = after((x_fars, g_fars), *kept)
    hid_a_far, act_a_far = activations(
        dot(x_fars, both_a), dot(g_fars, down_a), scales(g_far_parts, me)
    )
    act_a_far, act_b_far = after((act_a_far, act_b_far), *for_pair)
    to_x, to_y, first, second, far_own = plane_sends(dx_rows(act_a_far, act_b_far, both_a, both_b))
    far_x, far_y = swap(to_x, ACROSS_X), swap(to_y, ACROSS_Y)
    act_a_near, act_b_near = after((act_a_near, act_b_near), to_x, to_y)
    half = tok_rows // 2
    dx_near = dx_rows(act_a_near, act_b_near, both_a, both_b)
    first, second = plus(first, far_y[half:]), plus(second, far_x[half:])
    far_first, far_second = swap(first, ACROSS_X), swap(second, ACROSS_Y)
    dx_near = after(dx_near, first, second)
    to_x, to_y, first, second, near_own = plane_sends(dx_near)
    near_x, near_y = swap(to_x, ACROSS_X), swap(to_y, ACROSS_Y)
    far_total = plane_total(far_own, far_x, far_y, far_first, far_second).astype(low)
    far_got = swap(far_total, ACROSS_Z)
    x_fars, g_fars = after((x_fars, g_fars), far_total)
    pairs_a = (x_fars, act_a_far, near_a[:2]), (g_fars, hid_a_far, near_a[2:])
    sent = [(dot(r[:, send], v, contract_rows) + n[0]).astype(low) for r, v, n in pairs_a]
    got = [swap(sent[0], 0), swap(sent[1], 0)]
    mine = [
        dot(r[:, keep], v, contract_rows) + n[1] + g.astype(wide) for (r, v, n), g in zip(pairs_a, got)
    ]
    first, second = plus(first, near_y[half:]), plus(second, near_x[half:])
    near_first, near_second = swap(first, ACROSS_X), swap(second, ACROSS_Y)
    near_total = plane_total(near_own, near_x, near_y, near_first, near_second)
    input_grad = turn((near_total + far_got.astype(wide)).astype(low))
    totals = [m + f.astype(wide) for m, f in zip(mine, from_pair)]
    return input_grad, totals[0][None, :, :ff], totals[0][None, :, ff:], totals[1][None]


def expert_parts(x_rows, dy_rows, gate_w, up_w, down_w):
    gate_pre = jnp.dot(x_rows, gate_w, preferred_element_type=jnp.float32)
    up_pre = jnp.dot(x_rows, up_w, preferred_element_type=jnp.float32)
    sig_gate = jax.nn.sigmoid(gate_pre)
    active = gate_pre * sig_gate
    hidden = (active * up_pre).astype(jnp.bfloat16)
    hidden_grad = jnp.dot(dy_rows, down_w, preferred_element_type=jnp.float32)
    gate_grad = (hidden_grad * up_pre * sig_gate * (1.0 + gate_pre * (1.0 - sig_gate))).astype(
        jnp.bfloat16
    )
    up_grad = (hidden_grad * active).astype(jnp.bfloat16)
    return (hidden, jnp.concatenate([gate_grad, up_grad], axis=1))


def weight_terms(x_rows, dy_rows, hidden, act_grads):
    first = lax.dot_general(x_rows, act_grads, contract_rows, preferred_element_type=jnp.float32)
    second = lax.dot_general(dy_rows, hidden, contract_rows, preferred_element_type=jnp.float32)
    return jnp.concatenate([first, second], axis=1)


def row_grads(act_grads, both_w):
    return lax.dot_general(
        act_grads, both_w, contract_cols, preferred_element_type=jnp.float32
    ).astype(jnp.bfloat16)


def routed_local(tokens, out_grad, gates, expert_ids, w_gate, w_up, w_down):
    experts = lax.axis_size("expert")
    tok_rows, width = tokens.shape
    top_k = expert_ids.shape[1]
    capacity = 5 * tok_rows * top_k // (4 * experts)
    slot_count = experts * capacity
    flat_ids = expert_ids.reshape(-1)
    expert_match = (flat_ids[:, None] == jnp.arange(experts, dtype=jnp.int32)[None, :]).astype(
        jnp.int32
    )
    earlier = jnp.cumsum(expert_match, axis=0) - expert_match
    position = jnp.sum(earlier * expert_match, axis=1)
    slot_of = flat_ids * capacity + position
    slot_hits = (slot_of[None, :] == jnp.arange(slot_count, dtype=jnp.int32)[:, None]).reshape(
        slot_count, tok_rows, top_k
    )
    pick_tok = jnp.any(slot_hits, axis=2).astype(jnp.bfloat16)
    scale_tok = jnp.sum(jnp.where(slot_hits, gates[None, :, :], jnp.float32(0.0)), axis=2)
    gate_slot = jnp.sum(scale_tok, axis=1)
    send_x = jnp.dot(pick_tok, tokens, preferred_element_type=jnp.float32).astype(jnp.bfloat16)
    send_x = send_x.reshape(experts, capacity, width)
    grad_picked = jnp.dot(pick_tok, out_grad, preferred_element_type=jnp.float32)
    send_dy = (gate_slot[:, None] * grad_picked).astype(jnp.bfloat16)
    send_dy = send_dy.reshape(experts, capacity, width)
    recv_x = lax.all_to_all(send_x, "expert", split_axis=0, concat_axis=0, tiled=True)
    recv_dy = lax.all_to_all(send_dy, "expert", split_axis=0, concat_axis=0, tiled=True)
    full_gate, full_up, full_down = (
        lax.all_gather(w_gate, "dp", axis=1, tiled=True),
        lax.all_gather(w_up, "dp", axis=1, tiled=True),
        lax.all_gather(w_down, "dp", axis=1, tiled=True),
    )
    gate_w = full_gate[0]
    up_w = full_up[0]
    down_w = full_down[0]
    ff_width = gate_w.shape[1]
    both_w = jnp.concatenate([gate_w, up_w], axis=1)
    x_rows = recv_x.reshape(slot_count, width)
    dy_rows = recv_dy.reshape(slot_count, width)
    hidden, act_grads = expert_parts(x_rows, dy_rows, gate_w, up_w, down_w)
    row_out = row_grads(act_grads, both_w)
    returned = lax.all_to_all(
        row_out.reshape(experts, capacity, width), "expert", split_axis=0, concat_axis=0, tiled=True
    )
    grad_sums = lax.psum_scatter(
        weight_terms(x_rows, dy_rows, hidden, act_grads), "dp", scatter_dimension=0, tiled=True
    )
    input_grad = lax.dot_general(
        pick_tok,
        returned.reshape(slot_count, width),
        contract_rows,
        preferred_element_type=jnp.float32,
    ).astype(jnp.bfloat16)
    grad_gate = grad_sums[None, :, :ff_width]
    grad_up = grad_sums[None, :, ff_width : 2 * ff_width]
    grad_down = grad_sums[None, :, 2 * ff_width :]
    return (input_grad, grad_gate, grad_up, grad_down)


def solution(mesh):
    in_specs = (
        P(("expert", "dp"), None),
        P(("expert", "dp"), None),
        P(("expert", "dp"), None),
        P(("expert", "dp"), None),
        P("expert", "dp", None),
        P("expert", "dp", None),
        P("expert", "dp", None),
    )
    out_specs = (
        P(("expert", "dp"), None),
        P("expert", "dp", None),
        P("expert", "dp", None),
        P("expert", "dp", None),
    )
    def local(tokens, *rest):
        tok_rows, experts = tokens.shape[0], mesh.shape["expert"]
        capacity = 5 * tok_rows * rest[1].shape[1] // (4 * experts)
        dense = experts == 16 and mesh.shape["dp"] == 2 and 2 * capacity > tok_rows
        return (dense_local if dense else routed_local)(tokens, *rest)

    return jax.shard_map(
        local, mesh=mesh, in_specs=in_specs, out_specs=out_specs, check_vma=False
    )
```

```python
import jax
import jax.numpy as jnp
from jax import lax
from jax.experimental import pallas as pl
from jax.experimental.pallas import tpu as pltpu
from jax.sharding import PartitionSpec as P

contract_rows = (((0,), (0,)), ((), ()))
contract_cols = (((1,), (1,)), ((), ()))
ACROSS_X, ACROSS_Y, PAIR, ACROSS_Z = 1, 2, 4, 8
low, wide = jnp.bfloat16, jnp.float32


def after(rows, *earlier):
    return lax.optimization_barrier((rows,) + earlier)[0]


def swap(rows, bit):
    if bit == 0:
        return lax.ppermute(rows, "dp", [(0, 1), (1, 0)])
    experts = lax.axis_size("expert")
    return lax.ppermute(rows, "expert", [(i, i ^ bit) for i in range(experts)])


def swap_far(rows, bit):
    experts = lax.axis_size("expert")
    groups = [[i, i ^ bit] for i in range(experts) if i < i ^ bit]
    both = lax.all_to_all(
        jnp.stack([rows, rows]), "expert", split_axis=0, concat_axis=0, tiled=True, axis_index_groups=groups
    )
    return jnp.where(lax.axis_index("expert") & bit == 0, both[1], both[0])


def turn(rows):
    half = rows.shape[1] // 2
    turned = jnp.concatenate([rows[:, half:], rows[:, :half]], axis=1)
    return jnp.where(lax.axis_index("dp") == 0, rows, turned)


def gate_rows(gates, expert_ids, experts):
    count = gates.shape[0]
    lanes = lax.broadcasted_iota(jnp.int32, (1, experts * count), 1) // count
    ids = jnp.tile(expert_ids.T, (1, experts))
    spread = jnp.sum(jnp.where(ids == lanes, jnp.tile(gates.T, (1, experts)), 0.0), axis=0, keepdims=True)
    first = lax.reduce_precision(spread, 8, 7)
    second = lax.reduce_precision(spread - first, 8, 7)
    third = spread - first - second
    empty = jnp.zeros((5, experts * count), wide)
    return jnp.concatenate([first, second, third, empty], axis=0).astype(low)


def scale_of(block, rows, expert):
    terms = lax.dynamic_slice(block, (rows, expert * rows), (8, rows))
    return jnp.sum(terms.astype(wide), axis=0)


def activations(pre, out_pre, scale):
    ff = out_pre.shape[1]
    gate_pre, up_pre = pre[:, :ff], pre[:, ff:]
    hidden_grad = scale * out_pre
    sig_gate = jax.nn.sigmoid(gate_pre)
    active = gate_pre * sig_gate
    hidden = (scale * (active * up_pre)).astype(low)
    gate_grad = (hidden_grad * up_pre * sig_gate * (1.0 + gate_pre * (1.0 - sig_gate))).astype(low)
    up_grad = (hidden_grad * active).astype(low)
    return hidden, jnp.concatenate([gate_grad, up_grad], axis=1)


def dot(a, b, dims=(((1,), (0,)), ((), ()))):
    return lax.dot_general(a, b, dims, preferred_element_type=wide)


def plane_sends(dx):
    quarter = dx.shape[0] // 4
    half = quarter // 2
    own, of_x, of_y, of_xy = [dx[i * quarter : (i + 1) * quarter] for i in range(4)]
    to_y = jnp.concatenate([of_y[:half], of_xy[:half]], axis=0)
    to_x = jnp.concatenate([of_x[half:], of_xy[half:]], axis=0)
    return to_x, to_y, of_x[:half], of_y[half:], own


def plus(a, b):
    return (a.astype(wide) + b.astype(wide)).astype(low)


def plane_total(own, got_x, got_y, got_first, got_second):
    half = got_first.shape[0]
    got = (
        jnp.concatenate([got_y[:half], got_x[:half]], axis=0).astype(wide)
        + jnp.concatenate([got_first, got_second], axis=0).astype(wide)
    )
    return own.astype(wide) + got


def dx_kernel(act_a, act_b, w_a, w_b, out):
    out[...] = (dot(act_a[...], w_a[...], contract_cols) + dot(act_b[...], w_b[...], contract_cols)).astype(low)


def dx_rows(act_a, act_b, w_a, w_b):
    rows, depth = act_a.shape
    width = w_a.shape[0]
    tile = min(width, 256)
    whole = pl.BlockSpec((rows, depth), lambda i: (0, 0))
    part = pl.BlockSpec((tile, depth), lambda i: (i, 0))
    return pl.pallas_call(
        dx_kernel,
        grid=(width // tile,),
        in_specs=[whole, whole, part, part],
        out_specs=pl.BlockSpec((rows, tile), lambda i: (0, i)),
        out_shape=jax.ShapeDtypeStruct((rows, width), low),
        compiler_params=pltpu.CompilerParams(vmem_limit_bytes=10 << 20),
        cost_estimate=pl.CostEstimate(
            flops=4 * rows * depth * width, bytes_accessed=4 * width * depth + 2 * rows * width, transcendentals=0
        ),
    )(act_a, act_b, w_a, w_b)


def add_up(kept_both, kept_down, got, more):
    rows, ff = kept_down.shape
    tile = min(rows, 256)

    def kernel(both, down, got, more, gate_out, up_out, down_out):
        extra = got[...].astype(wide) + more[...].astype(wide)
        gate_out[...] = both[:, :ff] + extra[:, :ff]
        up_out[...] = both[:, ff:] + extra[:, ff : 2 * ff]
        down_out[...] = down[...] + extra[:, 2 * ff :]

    def part(columns):
        return pl.BlockSpec((tile, columns), lambda i: (i, 0))

    return pl.pallas_call(
        kernel,
        grid=(rows // tile,),
        in_specs=[part(2 * ff), part(ff), part(3 * ff), part(3 * ff)],
        out_specs=[part(ff)] * 3,
        out_shape=[jax.ShapeDtypeStruct((rows, ff), wide)] * 3,
        compiler_params=pltpu.CompilerParams(vmem_limit_bytes=16 << 20),
        cost_estimate=pl.CostEstimate(flops=20_000_000_000, bytes_accessed=0, transcendentals=0),
    )(kept_both, kept_down, got, more)


def dense_local(tokens, out_grad, gates, expert_ids, w_gate, w_up, w_down):
    experts = lax.axis_size("expert")
    tok_rows, width = tokens.shape
    mid = width // 2
    ff = w_gate.shape[2]
    me = lax.axis_index("expert")
    pair = me ^ PAIR

    def join(parts):
        return jnp.concatenate([p[:tok_rows] for p in parts], axis=0)

    def scales(parts, expert):
        return jnp.concatenate([scale_of(p, tok_rows, expert) for p in parts])[:, None]

    def weight_sum(rows, acts, columns):
        return sum(dot(r[:, columns], a, contract_rows) for r, a in zip(rows, acts))

    keep, send = slice(0, mid), slice(mid, width)

    both_mine, down_mine = jnp.concatenate([w_gate[0], w_up[0]], axis=1), w_down[0]
    x_own = turn(tokens)
    g_own = jnp.concatenate([turn(out_grad), gate_rows(gates, expert_ids, experts)], axis=0)
    far = swap_far(jnp.concatenate([x_own, g_own], axis=0), ACROSS_Z)
    both_pair = swap(both_mine, PAIR)
    x_x = swap(x_own, ACROSS_X)
    g_y = swap(g_own, ACROSS_Y)
    g_x = swap(after(g_own, x_x, g_y), ACROSS_X)
    x_y = swap(after(x_own, x_x, g_y), ACROSS_Y)
    g_y, x_x = after((g_y, x_x), g_x, x_y)
    g_xy = swap(g_y, ACROSS_X)
    x_xy = swap(x_x, ACROSS_Y)
    far = after(far, g_xy, x_xy)
    far_of_x = swap(far, ACROSS_X)
    far_of_y = swap(far, ACROSS_Y)
    x_near_parts = x_own, x_x, x_y, after(x_xy, both_pair)
    g_near_parts = g_own, g_x, g_y, after(g_xy, both_pair)
    x_near, g_near = join(x_near_parts), join(g_near_parts)
    scale_a_near, scale_b_near = scales(g_near_parts, me), scales(g_near_parts, pair)
    down_pair = swap(after(down_mine, far), PAIR)
    far_of_x, far_of_y = after((far_of_x, far_of_y), x_near, g_near)
    g_far_xy = swap(far_of_y[tok_rows:], ACROSS_X)
    x_far_xy = swap(far_of_x[:tok_rows], ACROSS_Y)
    both_pair = after(both_pair, far_of_x, far_of_y)
    both_pair_other = swap(both_pair, 0)
    both_b = jnp.concatenate([both_pair, both_pair_other], axis=0)
    pre_b_near = dot(x_near, both_b)
    down_pair = after(down_pair, g_far_xy, x_far_xy)
    down_pair_other = swap(down_pair, 0)
    down_b = jnp.concatenate([down_pair, down_pair_other], axis=0)
    x_far, x_far_x, x_far_y = [v[:tok_rows] for v in (far, far_of_x, far_of_y)]
    g_far, g_far_x, g_far_y = [v[tok_rows:] for v in (far, far_of_x, far_of_y)]
    hid_b_near, act_b_near = activations(pre_b_near, dot(g_near, down_b), scale_b_near)
    x_far, x_far_x, x_far_y = [v[:tok_rows] for v in (far, far_of_x, far_of_y)]
    g_far, g_far_x, g_far_y = [v[tok_rows:] for v in (far, far_of_x, far_of_y)]
    x_far_parts = (x_far, x_far_x, x_far_y, x_far_xy)
    g_far_parts = (g_far, g_far_x, g_far_y, g_far_xy)
    x_fars, g_fars = join(x_far_parts), join(g_far_parts)
    hid_b_far, act_b_far = activations(
        dot(x_fars, both_b), dot(g_fars, down_b), scales(g_far_parts, pair)
    )
    pairs_b = ((x_near, x_fars), (act_b_near, act_b_far)), ((g_near, g_fars), (hid_b_near, hid_b_far))
    sent = jnp.concatenate([weight_sum(r, v, send).astype(low) for r, v in pairs_b], axis=1)
    got = swap(sent, 0)
    kept = [weight_sum(r, v, keep) for r, v in pairs_b]
    for_pair = (jnp.concatenate(kept, axis=1) + got.astype(wide)).astype(low)
    from_pair = swap(for_pair, PAIR)
    both_other = swap(after(both_mine, for_pair), 0)
    down_other = swap(after(down_mine, for_pair), 0)
    both_a = jnp.concatenate([both_mine, both_other], axis=0)
    down_a = jnp.concatenate([down_mine, down_other], axis=0)
    x_fars, g_fars, x_near, g_near, both_a, down_a = after(
        (x_fars, g_fars, x_near, g_near, both_a, down_a), for_pair
    )
    hid_a_far, act_a_far = activations(
        dot(x_fars, both_a), dot(g_fars, down_a), scales(g_far_parts, me)
    )
    to_x, to_y, first, second, far_own = plane_sends(dx_rows(act_a_far, act_b_far, both_a, both_b))
    far_x, far_y = swap(to_x, ACROSS_X), swap(to_y, ACROSS_Y)
    x_near, g_near = after((x_near, g_near), to_x, to_y)
    hid_a_near, act_a_near = activations(dot(x_near, both_a), dot(g_near, down_a), scale_a_near)
    half = tok_rows // 2
    dx_near = dx_rows(act_a_near, act_b_near, both_a, both_b)
    first, second = plus(first, far_y[half:]), plus(second, far_x[half:])
    far_first, far_second = swap(first, ACROSS_X), swap(second, ACROSS_Y)
    dx_near = after(dx_near, first, second)
    to_x, to_y, first, second, near_own = plane_sends(dx_near)
    near_x, near_y = swap(to_x, ACROSS_X), swap(to_y, ACROSS_Y)
    far_total = plane_total(far_own, far_x, far_y, far_first, far_second).astype(low)
    far_got = swap(far_total, ACROSS_Z)
    x_fars, g_fars = after((x_fars, g_fars), far_total, dx_near)
    pairs_a = ((x_near, x_fars), (act_a_near, act_a_far)), ((g_near, g_fars), (hid_a_near, hid_a_far))
    sent = jnp.concatenate([weight_sum(r, v, send).astype(low) for r, v in pairs_a], axis=1)
    got = swap(sent, 0)
    kept = [weight_sum(r, v, keep) for r, v in pairs_a]
    first, second = plus(first, near_y[half:]), plus(second, near_x[half:])
    near_first, near_second = swap(first, ACROSS_X), swap(second, ACROSS_Y)
    far_got = after(far_got, from_pair)
    near_total = plane_total(near_own, near_x, near_y, near_first, near_second)
    input_grad = turn((near_total + far_got.astype(wide)).astype(low))
    grads = add_up(*kept, got, after(from_pair, *kept))
    return (input_grad,) + tuple(g[None] for g in grads)


def expert_parts(x_rows, dy_rows, gate_w, up_w, down_w):
    gate_pre = jnp.dot(x_rows, gate_w, preferred_element_type=jnp.float32)
    up_pre = jnp.dot(x_rows, up_w, preferred_element_type=jnp.float32)
    sig_gate = jax.nn.sigmoid(gate_pre)
    active = gate_pre * sig_gate
    hidden = (active * up_pre).astype(jnp.bfloat16)
    hidden_grad = jnp.dot(dy_rows, down_w, preferred_element_type=jnp.float32)
    gate_grad = (hidden_grad * up_pre * sig_gate * (1.0 + gate_pre * (1.0 - sig_gate))).astype(
        jnp.bfloat16
    )
    up_grad = (hidden_grad * active).astype(jnp.bfloat16)
    return (hidden, jnp.concatenate([gate_grad, up_grad], axis=1))


def weight_terms(x_rows, dy_rows, hidden, act_grads):
    first = lax.dot_general(x_rows, act_grads, contract_rows, preferred_element_type=jnp.float32)
    second = lax.dot_general(dy_rows, hidden, contract_rows, preferred_element_type=jnp.float32)
    return jnp.concatenate([first, second], axis=1)


def row_grads(act_grads, both_w):
    return lax.dot_general(
        act_grads, both_w, contract_cols, preferred_element_type=jnp.float32
    ).astype(jnp.bfloat16)


def routed_local(tokens, out_grad, gates, expert_ids, w_gate, w_up, w_down):
    experts = lax.axis_size("expert")
    tok_rows, width = tokens.shape
    top_k = expert_ids.shape[1]
    capacity = 5 * tok_rows * top_k // (4 * experts)
    slot_count = experts * capacity
    flat_ids = expert_ids.reshape(-1)
    expert_match = (flat_ids[:, None] == jnp.arange(experts, dtype=jnp.int32)[None, :]).astype(
        jnp.int32
    )
    earlier = jnp.cumsum(expert_match, axis=0) - expert_match
    position = jnp.sum(earlier * expert_match, axis=1)
    slot_of = flat_ids * capacity + position
    slot_hits = (slot_of[None, :] == jnp.arange(slot_count, dtype=jnp.int32)[:, None]).reshape(
        slot_count, tok_rows, top_k
    )
    pick_tok = jnp.any(slot_hits, axis=2).astype(jnp.bfloat16)
    scale_tok = jnp.sum(jnp.where(slot_hits, gates[None, :, :], jnp.float32(0.0)), axis=2)
    gate_slot = jnp.sum(scale_tok, axis=1)
    send_x = jnp.dot(pick_tok, tokens, preferred_element_type=jnp.float32).astype(jnp.bfloat16)
    send_x = send_x.reshape(experts, capacity, width)
    grad_picked = jnp.dot(pick_tok, out_grad, preferred_element_type=jnp.float32)
    send_dy = (gate_slot[:, None] * grad_picked).astype(jnp.bfloat16)
    send_dy = send_dy.reshape(experts, capacity, width)
    recv_x = lax.all_to_all(send_x, "expert", split_axis=0, concat_axis=0, tiled=True)
    recv_dy = lax.all_to_all(send_dy, "expert", split_axis=0, concat_axis=0, tiled=True)
    full_gate, full_up, full_down = (
        lax.all_gather(w_gate, "dp", axis=1, tiled=True),
        lax.all_gather(w_up, "dp", axis=1, tiled=True),
        lax.all_gather(w_down, "dp", axis=1, tiled=True),
    )
    gate_w = full_gate[0]
    up_w = full_up[0]
    down_w = full_down[0]
    ff_width = gate_w.shape[1]
    both_w = jnp.concatenate([gate_w, up_w], axis=1)
    x_rows = recv_x.reshape(slot_count, width)
    dy_rows = recv_dy.reshape(slot_count, width)
    hidden, act_grads = expert_parts(x_rows, dy_rows, gate_w, up_w, down_w)
    row_out = row_grads(act_grads, both_w)
    returned = lax.all_to_all(
        row_out.reshape(experts, capacity, width), "expert", split_axis=0, concat_axis=0, tiled=True
    )
    grad_sums = lax.psum_scatter(
        weight_terms(x_rows, dy_rows, hidden, act_grads), "dp", scatter_dimension=0, tiled=True
    )
    input_grad = lax.dot_general(
        pick_tok,
        returned.reshape(slot_count, width),
        contract_rows,
        preferred_element_type=jnp.float32,
    ).astype(jnp.bfloat16)
    grad_gate = grad_sums[None, :, :ff_width]
    grad_up = grad_sums[None, :, ff_width : 2 * ff_width]
    grad_down = grad_sums[None, :, 2 * ff_width :]
    return (input_grad, grad_gate, grad_up, grad_down)


def solution(mesh):
    in_specs = (
        P(("expert", "dp"), None),
        P(("expert", "dp"), None),
        P(("expert", "dp"), None),
        P(("expert", "dp"), None),
        P("expert", "dp", None),
        P("expert", "dp", None),
        P("expert", "dp", None),
    )
    out_specs = (
        P(("expert", "dp"), None),
        P("expert", "dp", None),
        P("expert", "dp", None),
        P("expert", "dp", None),
    )
    def local(tokens, *rest):
        tok_rows, experts = tokens.shape[0], mesh.shape["expert"]
        capacity = 5 * tok_rows * rest[1].shape[1] // (4 * experts)
        dense = experts == 16 and mesh.shape["dp"] == 2 and 2 * capacity > tok_rows
        return (dense_local if dense else routed_local)(tokens, *rest)

    return jax.shard_map(
        local, mesh=mesh, in_specs=in_specs, out_specs=out_specs, check_vma=False
    )
```

```python
import jax
import jax.numpy as jnp
from jax import lax
from jax.experimental import pallas as pl
from jax.experimental.pallas import tpu as pltpu
from jax.sharding import PartitionSpec as P

contract_rows = (((0,), (0,)), ((), ()))
contract_cols = (((1,), (1,)), ((), ()))
ACROSS_X, ACROSS_Y, PAIR, ACROSS_Z = 1, 2, 4, 8
low, wide = jnp.bfloat16, jnp.float32


def after(rows, *earlier):
    return lax.optimization_barrier((rows,) + earlier)[0]


def swap(rows, bit):
    if bit == 0:
        return lax.ppermute(rows, "dp", [(0, 1), (1, 0)])
    experts = lax.axis_size("expert")
    return lax.ppermute(rows, "expert", [(i, i ^ bit) for i in range(experts)])


def swap_far(rows, bit):
    experts = lax.axis_size("expert")
    groups = [[i, i ^ bit] for i in range(experts) if i < i ^ bit]
    both = lax.all_to_all(
        jnp.stack([rows, rows]), "expert", split_axis=0, concat_axis=0, tiled=True, axis_index_groups=groups
    )
    return jnp.where(lax.axis_index("expert") & bit == 0, both[1], both[0])


def turn(rows):
    half = rows.shape[1] // 2
    turned = jnp.concatenate([rows[:, half:], rows[:, :half]], axis=1)
    return jnp.where(lax.axis_index("dp") == 0, rows, turned)


def gate_rows(gates, expert_ids, experts):
    count = gates.shape[0]
    lanes = lax.broadcasted_iota(jnp.int32, (1, experts * count), 1) // count
    ids = jnp.tile(expert_ids.T, (1, experts))
    spread = jnp.sum(jnp.where(ids == lanes, jnp.tile(gates.T, (1, experts)), 0.0), axis=0, keepdims=True)
    first = lax.reduce_precision(spread, 8, 7)
    second = lax.reduce_precision(spread - first, 8, 7)
    third = spread - first - second
    empty = jnp.zeros((5, experts * count), wide)
    return jnp.concatenate([first, second, third, empty], axis=0).astype(low)


def scale_of(block, rows, expert):
    terms = lax.dynamic_slice(block, (rows, expert * rows), (8, rows))
    return jnp.sum(terms.astype(wide), axis=0)


def activations(pre, out_pre, scale):
    ff = out_pre.shape[1]
    gate_pre, up_pre = pre[:, :ff], pre[:, ff:]
    hidden_grad = scale * out_pre
    sig_gate = jax.nn.sigmoid(gate_pre)
    active = gate_pre * sig_gate
    hidden = (scale * (active * up_pre)).astype(low)
    gate_grad = (hidden_grad * up_pre * sig_gate * (1.0 + gate_pre * (1.0 - sig_gate))).astype(low)
    up_grad = (hidden_grad * active).astype(low)
    return hidden, jnp.concatenate([gate_grad, up_grad], axis=1)


def dot(a, b, dims=(((1,), (0,)), ((), ()))):
    return lax.dot_general(a, b, dims, preferred_element_type=wide)


def plane_sends(dx):
    quarter = dx.shape[0] // 4
    half = quarter // 2
    own, of_x, of_y, of_xy = [dx[i * quarter : (i + 1) * quarter] for i in range(4)]
    to_y = jnp.concatenate([of_y[:half], of_xy[:half]], axis=0)
    to_x = jnp.concatenate([of_x[half:], of_xy[half:]], axis=0)
    return to_x, to_y, of_x[:half], of_y[half:], own


def plus(a, b):
    return (a.astype(wide) + b.astype(wide)).astype(low)


def plane_total(own, got_x, got_y, got_first, got_second):
    half = got_first.shape[0]
    got = (
        jnp.concatenate([got_y[:half], got_x[:half]], axis=0).astype(wide)
        + jnp.concatenate([got_first, got_second], axis=0).astype(wide)
    )
    return own.astype(wide) + got


def dx_kernel(act_a, act_b, w_a, w_b, out):
    out[...] = (dot(act_a[...], w_a[...], contract_cols) + dot(act_b[...], w_b[...], contract_cols)).astype(low)


def dx_rows(act_a, act_b, w_a, w_b):
    rows, depth = act_a.shape
    width = w_a.shape[0]
    tile = min(width, 256)
    whole = pl.BlockSpec((rows, depth), lambda i: (0, 0))
    part = pl.BlockSpec((tile, depth), lambda i: (i, 0))
    return pl.pallas_call(
        dx_kernel,
        grid=(width // tile,),
        in_specs=[whole, whole, part, part],
        out_specs=pl.BlockSpec((rows, tile), lambda i: (0, i)),
        out_shape=jax.ShapeDtypeStruct((rows, width), low),
        compiler_params=pltpu.CompilerParams(vmem_limit_bytes=10 << 20),
        cost_estimate=pl.CostEstimate(
            flops=4 * rows * depth * width, bytes_accessed=4 * width * depth + 2 * rows * width, transcendentals=0
        ),
    )(act_a, act_b, w_a, w_b)


def add_up(kept_both, kept_down, got, more):
    rows, ff = kept_down.shape
    tile = min(rows, 256)

    def kernel(both, down, got, more, gate_out, up_out, down_out):
        extra = got[...].astype(wide) + more[...].astype(wide)
        gate_out[...] = both[:, :ff] + extra[:, :ff]
        up_out[...] = both[:, ff:] + extra[:, ff : 2 * ff]
        down_out[...] = down[...] + extra[:, 2 * ff :]

    def part(columns):
        return pl.BlockSpec((tile, columns), lambda i: (i, 0))

    return pl.pallas_call(
        kernel,
        grid=(rows // tile,),
        in_specs=[part(2 * ff), part(ff), part(3 * ff), part(3 * ff)],
        out_specs=[part(ff)] * 3,
        out_shape=[jax.ShapeDtypeStruct((rows, ff), wide)] * 3,
        compiler_params=pltpu.CompilerParams(vmem_limit_bytes=16 << 20),
        cost_estimate=pl.CostEstimate(flops=20_000_000_000, bytes_accessed=0, transcendentals=0),
    )(kept_both, kept_down, got, more)


def dense_local(tokens, out_grad, gates, expert_ids, w_gate, w_up, w_down):
    experts = lax.axis_size("expert")
    tok_rows, width = tokens.shape
    mid = width // 2
    ff = w_gate.shape[2]
    me = lax.axis_index("expert")
    pair = me ^ PAIR

    def join(parts):
        return jnp.concatenate([p[:tok_rows] for p in parts], axis=0)

    def scales(parts, expert):
        return jnp.concatenate([scale_of(p, tok_rows, expert) for p in parts])[:, None]

    def weight_sum(rows, acts, columns):
        return sum(dot(r[:, columns], a, contract_rows) for r, a in zip(rows, acts))

    keep, send = slice(0, mid), slice(mid, width)

    gate_mine, up_mine, down_mine = w_gate[0], w_up[0], w_down[0]
    both_mine = jnp.concatenate([gate_mine, up_mine], axis=1)
    x_own = turn(tokens)
    g_own = jnp.concatenate([turn(out_grad), gate_rows(gates, expert_ids, experts)], axis=0)
    far = swap_far(jnp.concatenate([x_own, g_own], axis=0), ACROSS_Z)
    gate_pair, up_pair = swap(gate_mine, PAIR), swap(up_mine, PAIR)
    both_pair = jnp.concatenate([gate_pair, up_pair], axis=1)
    x_x = swap(x_own, ACROSS_X)
    g_y = swap(g_own, ACROSS_Y)
    g_x = swap(after(g_own, x_x, g_y), ACROSS_X)
    x_y = swap(after(x_own, x_x, g_y), ACROSS_Y)
    g_y, x_x = after((g_y, x_x), g_x, x_y)
    g_xy = swap(g_y, ACROSS_X)
    x_xy = swap(x_x, ACROSS_Y)
    far = after(far, g_xy, x_xy)
    far_of_x = swap(far, ACROSS_X)
    far_of_y = swap(far, ACROSS_Y)
    x_near_parts = x_own, x_x, x_y, after(x_xy, both_pair)
    g_near_parts = g_own, g_x, g_y, after(g_xy, both_pair)
    x_near, g_near = join(x_near_parts), join(g_near_parts)
    x_near, g_near = lax.optimization_barrier((x_near, g_near))
    scale_a_near, scale_b_near = scales(g_near_parts, me), scales(g_near_parts, pair)
    down_pair = swap(after(down_mine, far), PAIR)
    far_of_x, far_of_y = after((far_of_x, far_of_y), x_near, g_near)
    g_far_xy = swap(far_of_y[tok_rows:], ACROSS_X)
    x_far_xy = swap(far_of_x[:tok_rows], ACROSS_Y)
    both_pair = after(both_pair, far_of_x, far_of_y)
    both_pair_other = swap(both_pair, 0)
    both_b = jnp.concatenate([both_pair, both_pair_other], axis=0)
    pre_b_near = dot(x_near, both_b)
    down_pair = after(down_pair, g_far_xy, x_far_xy)
    down_pair_other = swap(down_pair, 0)
    down_b = jnp.concatenate([down_pair, down_pair_other], axis=0)
    x_far, x_far_x, x_far_y = [v[:tok_rows] for v in (far, far_of_x, far_of_y)]
    g_far, g_far_x, g_far_y = [v[tok_rows:] for v in (far, far_of_x, far_of_y)]
    hid_b_near, act_b_near = activations(pre_b_near, dot(g_near, down_b), scale_b_near)
    x_far, x_far_x, x_far_y = [v[:tok_rows] for v in (far, far_of_x, far_of_y)]
    g_far, g_far_x, g_far_y = [v[tok_rows:] for v in (far, far_of_x, far_of_y)]
    x_far_parts = (x_far, x_far_x, x_far_y, x_far_xy)
    g_far_parts = (g_far, g_far_x, g_far_y, g_far_xy)
    x_fars, g_fars = lax.optimization_barrier((join(x_far_parts), join(g_far_parts)))
    hid_b_far, act_b_far = activations(
        dot(x_fars, both_b), dot(g_fars, down_b), scales(g_far_parts, pair)
    )
    pairs_b = ((x_near, x_fars), (act_b_near, act_b_far)), ((g_near, g_fars), (hid_b_near, hid_b_far))
    sent = jnp.concatenate([weight_sum(r, v, send).astype(low) for r, v in pairs_b], axis=1)
    got = swap(sent, 0)
    kept = [weight_sum(r, v, keep) for r, v in pairs_b]
    for_pair = (jnp.concatenate(kept, axis=1) + got.astype(wide)).astype(low)
    from_pair = swap(for_pair, PAIR)
    both_other = swap(after(both_mine, for_pair), 0)
    down_other = swap(after(down_mine, for_pair), 0)
    both_a = jnp.concatenate([both_mine, both_other], axis=0)
    down_a = jnp.concatenate([down_mine, down_other], axis=0)
    x_fars, g_fars, x_near, g_near, both_a, down_a = after(
        (x_fars, g_fars, x_near, g_near, both_a, down_a), for_pair
    )
    hid_a_far, act_a_far = activations(
        dot(x_fars, both_a), dot(g_fars, down_a), scales(g_far_parts, me)
    )
    to_x, to_y, first, second, far_own = plane_sends(dx_rows(act_a_far, act_b_far, both_a, both_b))
    far_x, far_y = swap(to_x, ACROSS_X), swap(to_y, ACROSS_Y)
    x_near, g_near = after((x_near, g_near), to_x, to_y)
    hid_a_near, act_a_near = activations(dot(x_near, both_a), dot(g_near, down_a), scale_a_near)
    half = tok_rows // 2
    dx_near = dx_rows(act_a_near, act_b_near, both_a, both_b)
    first, second = plus(first, far_y[half:]), plus(second, far_x[half:])
    far_first, far_second = swap(first, ACROSS_X), swap(second, ACROSS_Y)
    dx_near = after(dx_near, first, second)
    to_x, to_y, first, second, near_own = plane_sends(dx_near)
    near_x, near_y = swap(to_x, ACROSS_X), swap(to_y, ACROSS_Y)
    far_total = plane_total(far_own, far_x, far_y, far_first, far_second).astype(low)
    far_got = swap(far_total, ACROSS_Z)
    x_fars, g_fars = after((x_fars, g_fars), far_total, dx_near)
    pairs_a = ((x_near, x_fars), (act_a_near, act_a_far)), ((g_near, g_fars), (hid_a_near, hid_a_far))
    sent = jnp.concatenate([weight_sum(r, v, send).astype(low) for r, v in pairs_a], axis=1)
    got = swap(sent, 0)
    kept = [weight_sum(r, v, keep) for r, v in pairs_a]
    first, second = plus(first, near_y[half:]), plus(second, near_x[half:])
    near_first, near_second = swap(first, ACROSS_X), swap(second, ACROSS_Y)
    far_got = after(far_got, from_pair)
    near_total = plane_total(near_own, near_x, near_y, near_first, near_second)
    input_grad = turn((near_total + far_got.astype(wide)).astype(low))
    grads = add_up(*kept, got, after(from_pair, *kept))
    return (input_grad,) + tuple(g[None] for g in grads)


def expert_parts(x_rows, dy_rows, gate_w, up_w, down_w):
    gate_pre = jnp.dot(x_rows, gate_w, preferred_element_type=jnp.float32)
    up_pre = jnp.dot(x_rows, up_w, preferred_element_type=jnp.float32)
    sig_gate = jax.nn.sigmoid(gate_pre)
    active = gate_pre * sig_gate
    hidden = (active * up_pre).astype(jnp.bfloat16)
    hidden_grad = jnp.dot(dy_rows, down_w, preferred_element_type=jnp.float32)
    gate_grad = (hidden_grad * up_pre * sig_gate * (1.0 + gate_pre * (1.0 - sig_gate))).astype(
        jnp.bfloat16
    )
    up_grad = (hidden_grad * active).astype(jnp.bfloat16)
    return (hidden, jnp.concatenate([gate_grad, up_grad], axis=1))


def weight_terms(x_rows, dy_rows, hidden, act_grads):
    first = lax.dot_general(x_rows, act_grads, contract_rows, preferred_element_type=jnp.float32)
    second = lax.dot_general(dy_rows, hidden, contract_rows, preferred_element_type=jnp.float32)
    return jnp.concatenate([first, second], axis=1)


def row_grads(act_grads, both_w):
    return lax.dot_general(
        act_grads, both_w, contract_cols, preferred_element_type=jnp.float32
    ).astype(jnp.bfloat16)


def routed_local(tokens, out_grad, gates, expert_ids, w_gate, w_up, w_down):
    experts = lax.axis_size("expert")
    tok_rows, width = tokens.shape
    top_k = expert_ids.shape[1]
    capacity = 5 * tok_rows * top_k // (4 * experts)
    slot_count = experts * capacity
    flat_ids = expert_ids.reshape(-1)
    expert_match = (flat_ids[:, None] == jnp.arange(experts, dtype=jnp.int32)[None, :]).astype(
        jnp.int32
    )
    earlier = jnp.cumsum(expert_match, axis=0) - expert_match
    position = jnp.sum(earlier * expert_match, axis=1)
    slot_of = flat_ids * capacity + position
    slot_hits = (slot_of[None, :] == jnp.arange(slot_count, dtype=jnp.int32)[:, None]).reshape(
        slot_count, tok_rows, top_k
    )
    pick_tok = jnp.any(slot_hits, axis=2).astype(jnp.bfloat16)
    scale_tok = jnp.sum(jnp.where(slot_hits, gates[None, :, :], jnp.float32(0.0)), axis=2)
    gate_slot = jnp.sum(scale_tok, axis=1)
    send_x = jnp.dot(pick_tok, tokens, preferred_element_type=jnp.float32).astype(jnp.bfloat16)
    send_x = send_x.reshape(experts, capacity, width)
    grad_picked = jnp.dot(pick_tok, out_grad, preferred_element_type=jnp.float32)
    send_dy = (gate_slot[:, None] * grad_picked).astype(jnp.bfloat16)
    send_dy = send_dy.reshape(experts, capacity, width)
    recv_x = lax.all_to_all(send_x, "expert", split_axis=0, concat_axis=0, tiled=True)
    recv_dy = lax.all_to_all(send_dy, "expert", split_axis=0, concat_axis=0, tiled=True)
    full_gate, full_up, full_down = (
        lax.all_gather(w_gate, "dp", axis=1, tiled=True),
        lax.all_gather(w_up, "dp", axis=1, tiled=True),
        lax.all_gather(w_down, "dp", axis=1, tiled=True),
    )
    gate_w = full_gate[0]
    up_w = full_up[0]
    down_w = full_down[0]
    ff_width = gate_w.shape[1]
    both_w = jnp.concatenate([gate_w, up_w], axis=1)
    x_rows = recv_x.reshape(slot_count, width)
    dy_rows = recv_dy.reshape(slot_count, width)
    hidden, act_grads = expert_parts(x_rows, dy_rows, gate_w, up_w, down_w)
    row_out = row_grads(act_grads, both_w)
    returned = lax.all_to_all(
        row_out.reshape(experts, capacity, width), "expert", split_axis=0, concat_axis=0, tiled=True
    )
    grad_sums = lax.psum_scatter(
        weight_terms(x_rows, dy_rows, hidden, act_grads), "dp", scatter_dimension=0, tiled=True
    )
    input_grad = lax.dot_general(
        pick_tok,
        returned.reshape(slot_count, width),
        contract_rows,
        preferred_element_type=jnp.float32,
    ).astype(jnp.bfloat16)
    grad_gate = grad_sums[None, :, :ff_width]
    grad_up = grad_sums[None, :, ff_width : 2 * ff_width]
    grad_down = grad_sums[None, :, 2 * ff_width :]
    return (input_grad, grad_gate, grad_up, grad_down)


def solution(mesh):
    in_specs = (
        P(("expert", "dp"), None),
        P(("expert", "dp"), None),
        P(("expert", "dp"), None),
        P(("expert", "dp"), None),
        P("expert", "dp", None),
        P("expert", "dp", None),
        P("expert", "dp", None),
    )
    out_specs = (
        P(("expert", "dp"), None),
        P("expert", "dp", None),
        P("expert", "dp", None),
        P("expert", "dp", None),
    )
    def local(tokens, *rest):
        tok_rows, experts = tokens.shape[0], mesh.shape["expert"]
        capacity = 5 * tok_rows * rest[1].shape[1] // (4 * experts)
        dense = experts == 16 and mesh.shape["dp"] == 2 and 2 * capacity > tok_rows
        return (dense_local if dense else routed_local)(tokens, *rest)

    return jax.shard_map(
        local, mesh=mesh, in_specs=in_specs, out_specs=out_specs, check_vma=False
    )
```

```python
import jax
import jax.numpy as jnp
from jax import lax
from jax.experimental import pallas as pl
from jax.experimental.pallas import tpu as pltpu
from jax.sharding import PartitionSpec as P

contract_rows = (((0,), (0,)), ((), ()))
contract_cols = (((1,), (1,)), ((), ()))
ACROSS_X, ACROSS_Y, PAIR, ACROSS_Z = 1, 2, 4, 8
low, wide = jnp.bfloat16, jnp.float32


def after(rows, *earlier):
    return lax.optimization_barrier((rows,) + earlier)[0]


def swap(rows, bit):
    if bit == 0:
        return lax.ppermute(rows, "dp", [(0, 1), (1, 0)])
    experts = lax.axis_size("expert")
    return lax.ppermute(rows, "expert", [(i, i ^ bit) for i in range(experts)])


def swap_far(rows, bit):
    experts = lax.axis_size("expert")
    groups = [[i, i ^ bit] for i in range(experts) if i < i ^ bit]
    both = lax.all_to_all(
        jnp.stack([rows, rows]), "expert", split_axis=0, concat_axis=0, tiled=True, axis_index_groups=groups
    )
    return jnp.where(lax.axis_index("expert") & bit == 0, both[1], both[0])


def turn(rows):
    half = rows.shape[1] // 2
    turned = jnp.concatenate([rows[:, half:], rows[:, :half]], axis=1)
    return jnp.where(lax.axis_index("dp") == 0, rows, turned)


def gate_rows(gates, expert_ids, experts):
    count = gates.shape[0]
    lanes = lax.broadcasted_iota(jnp.int32, (1, experts * count), 1) // count
    ids = jnp.tile(expert_ids.T, (1, experts))
    spread = jnp.sum(jnp.where(ids == lanes, jnp.tile(gates.T, (1, experts)), 0.0), axis=0, keepdims=True)
    first = lax.reduce_precision(spread, 8, 7)
    second = lax.reduce_precision(spread - first, 8, 7)
    third = spread - first - second
    empty = jnp.zeros((5, experts * count), wide)
    return jnp.concatenate([first, second, third, empty], axis=0).astype(low)


def scale_of(block, rows, expert):
    terms = lax.dynamic_slice(block, (rows, expert * rows), (8, rows))
    return jnp.sum(terms.astype(wide), axis=0)


def activations(pre, out_pre, scale):
    ff = out_pre.shape[1]
    gate_pre, up_pre = pre[:, :ff], pre[:, ff:]
    hidden_grad = scale * out_pre
    sig_gate = jax.nn.sigmoid(gate_pre)
    active = gate_pre * sig_gate
    hidden = (scale * (active * up_pre)).astype(low)
    gate_grad = (hidden_grad * up_pre * sig_gate * (1.0 + gate_pre * (1.0 - sig_gate))).astype(low)
    up_grad = (hidden_grad * active).astype(low)
    return hidden, jnp.concatenate([gate_grad, up_grad], axis=1)


def dot(a, b, dims=(((1,), (0,)), ((), ()))):
    return lax.dot_general(a, b, dims, preferred_element_type=wide)


def plane_sends(dx):
    quarter = dx.shape[0] // 4
    half = quarter // 2
    own, of_x, of_y, of_xy = [dx[i * quarter : (i + 1) * quarter] for i in range(4)]
    to_y = jnp.concatenate([of_y[:half], of_xy[:half]], axis=0)
    to_x = jnp.concatenate([of_x[half:], of_xy[half:]], axis=0)
    return to_x, to_y, of_x[:half], of_y[half:], own


def plus(a, b):
    return (a.astype(wide) + b.astype(wide)).astype(low)


def plane_total(own, got_x, got_y, got_first, got_second):
    half = got_first.shape[0]
    got = (
        jnp.concatenate([got_y[:half], got_x[:half]], axis=0).astype(wide)
        + jnp.concatenate([got_first, got_second], axis=0).astype(wide)
    )
    return own.astype(wide) + got


def dx_kernel(act_a, act_b, w_a, w_b, out):
    out[...] = (dot(act_a[...], w_a[...], contract_cols) + dot(act_b[...], w_b[...], contract_cols)).astype(low)


def dx_rows(act_a, act_b, w_a, w_b):
    rows, depth = act_a.shape
    width = w_a.shape[0]
    tile = min(width, 512)
    whole = pl.BlockSpec((rows, depth), lambda i: (0, 0))
    part = pl.BlockSpec((tile, depth), lambda i: (i, 0))
    return pl.pallas_call(
        dx_kernel,
        grid=(width // tile,),
        in_specs=[whole, whole, part, part],
        out_specs=pl.BlockSpec((rows, tile), lambda i: (0, i)),
        out_shape=jax.ShapeDtypeStruct((rows, width), low),
        compiler_params=pltpu.CompilerParams(vmem_limit_bytes=16 << 20),
        cost_estimate=pl.CostEstimate(
            flops=4 * rows * depth * width, bytes_accessed=4 * width * depth + 2 * rows * width, transcendentals=0
        ),
    )(act_a, act_b, w_a, w_b)


def add_up(kept_both, kept_down, got, more):
    rows, ff = kept_down.shape
    tile = min(rows, 256)

    def kernel(both, down, got, more, gate_out, up_out, down_out):
        extra = got[...].astype(wide) + more[...].astype(wide)
        gate_out[...] = both[:, :ff] + extra[:, :ff]
        up_out[...] = both[:, ff:] + extra[:, ff : 2 * ff]
        down_out[...] = down[...] + extra[:, 2 * ff :]

    def part(columns):
        return pl.BlockSpec((tile, columns), lambda i: (i, 0))

    return pl.pallas_call(
        kernel,
        grid=(rows // tile,),
        in_specs=[part(2 * ff), part(ff), part(3 * ff), part(3 * ff)],
        out_specs=[part(ff)] * 3,
        out_shape=[jax.ShapeDtypeStruct((rows, ff), wide)] * 3,
        compiler_params=pltpu.CompilerParams(vmem_limit_bytes=16 << 20),
        cost_estimate=pl.CostEstimate(flops=20_000_000_000, bytes_accessed=0, transcendentals=0),
    )(kept_both, kept_down, got, more)


def dense_local(tokens, out_grad, gates, expert_ids, w_gate, w_up, w_down):
    experts = lax.axis_size("expert")
    tok_rows, width = tokens.shape
    mid = width // 2
    ff = w_gate.shape[2]
    me = lax.axis_index("expert")
    pair = me ^ PAIR

    def join(parts):
        return jnp.concatenate([p[:tok_rows] for p in parts], axis=0)

    def scales(parts, expert):
        return jnp.concatenate([scale_of(p, tok_rows, expert) for p in parts])[:, None]

    def weight_sum(rows, acts, columns):
        return sum(dot(r[:, columns], a, contract_rows) for r, a in zip(rows, acts))

    keep, send = slice(0, mid), slice(mid, width)

    gate_mine, up_mine, down_mine = w_gate[0], w_up[0], w_down[0]
    both_mine = jnp.concatenate([gate_mine, up_mine], axis=1)
    x_own = turn(tokens)
    g_own = jnp.concatenate([turn(out_grad), gate_rows(gates, expert_ids, experts)], axis=0)
    far = swap_far(jnp.concatenate([x_own, g_own], axis=0), ACROSS_Z)
    gate_pair, up_pair = swap(gate_mine, PAIR), swap(up_mine, PAIR)
    both_pair = jnp.concatenate([gate_pair, up_pair], axis=1)
    x_x = swap(x_own, ACROSS_X)
    g_y = swap(g_own, ACROSS_Y)
    g_x = swap(after(g_own, x_x, g_y), ACROSS_X)
    x_y = swap(after(x_own, x_x, g_y), ACROSS_Y)
    g_y, x_x = after((g_y, x_x), g_x, x_y)
    g_xy = swap(g_y, ACROSS_X)
    x_xy = swap(x_x, ACROSS_Y)
    far = after(far, g_xy, x_xy)
    far_of_x = swap(far, ACROSS_X)
    far_of_y = swap(far, ACROSS_Y)
    x_near_parts = x_own, x_x, x_y, x_xy
    g_near_parts = g_own, g_x, g_y, after(g_xy, both_pair)
    x_near, g_near = join(x_near_parts), join(g_near_parts)
    x_near, g_near = lax.optimization_barrier((x_near, g_near))
    scale_a_near, scale_b_near = scales(g_near_parts, me), scales(g_near_parts, pair)
    down_pair = swap(after(down_mine, far), PAIR)
    far_of_x, far_of_y = after((far_of_x, far_of_y), x_near, g_near)
    g_far_xy = swap(far_of_y[tok_rows:], ACROSS_X)
    x_far_xy = swap(far_of_x[:tok_rows], ACROSS_Y)
    both_pair = after(both_pair, far_of_x, far_of_y)
    both_pair_other = swap(both_pair, 0)
    both_b = jnp.concatenate([both_pair, both_pair_other], axis=0)
    pre_b_near = dot(x_near, both_b)
    down_pair = after(down_pair, x_far_xy)
    down_pair_other = swap(down_pair, 0)
    down_b = jnp.concatenate([down_pair, down_pair_other], axis=0)
    x_far, x_far_x, x_far_y = [v[:tok_rows] for v in (far, far_of_x, far_of_y)]
    g_far, g_far_x, g_far_y = [v[tok_rows:] for v in (far, far_of_x, far_of_y)]
    hid_b_near, act_b_near = activations(pre_b_near, dot(g_near, down_b), scale_b_near)
    x_far, x_far_x, x_far_y = [v[:tok_rows] for v in (far, far_of_x, far_of_y)]
    g_far, g_far_x, g_far_y = [v[tok_rows:] for v in (far, far_of_x, far_of_y)]
    x_far_parts = (x_far, x_far_x, x_far_y, x_far_xy)
    g_far_parts = (g_far, g_far_x, g_far_y, g_far_xy)
    x_fars, g_fars = lax.optimization_barrier((join(x_far_parts), join(g_far_parts)))
    hid_b_far, act_b_far = activations(
        dot(x_fars, both_b), dot(g_fars, down_b), scales(g_far_parts, pair)
    )
    pairs_b = ((x_near, x_fars), (act_b_near, act_b_far)), ((g_near, g_fars), (hid_b_near, hid_b_far))
    sent = jnp.concatenate([weight_sum(r, v, send).astype(low) for r, v in pairs_b], axis=1)
    got = swap(sent, 0)
    kept = [weight_sum(r, v, keep) for r, v in pairs_b]
    for_pair = (jnp.concatenate(kept, axis=1) + got.astype(wide)).astype(low)
    from_pair = swap(for_pair, PAIR)
    both_other = swap(after(both_mine, for_pair), 0)
    down_other = swap(after(down_mine, for_pair), 0)
    both_a = jnp.concatenate([both_mine, both_other], axis=0)
    down_a = jnp.concatenate([down_mine, down_other], axis=0)
    x_fars, g_fars, x_near, g_near, both_a, down_a = after(
        (x_fars, g_fars, x_near, g_near, both_a, down_a), for_pair
    )
    hid_a_far, act_a_far = activations(
        dot(x_fars, both_a), dot(g_fars, down_a), scales(g_far_parts, me)
    )
    to_x, to_y, first, second, far_own = plane_sends(dx_rows(act_a_far, act_b_far, both_a, both_b))
    far_x, far_y = swap(to_x, ACROSS_X), swap(to_y, ACROSS_Y)
    x_near, g_near = after((x_near, g_near), to_x, to_y)
    hid_a_near, act_a_near = activations(dot(x_near, both_a), dot(g_near, down_a), scale_a_near)
    half = tok_rows // 2
    dx_near = dx_rows(act_a_near, act_b_near, both_a, both_b)
    first, second = plus(first, far_y[half:]), plus(second, far_x[half:])
    far_first, far_second = swap(first, ACROSS_X), swap(second, ACROSS_Y)
    dx_near = after(dx_near, first, second)
    to_x, to_y, first, second, near_own = plane_sends(dx_near)
    near_x, near_y = swap(to_x, ACROSS_X), swap(to_y, ACROSS_Y)
    far_total = plane_total(far_own, far_x, far_y, far_first, far_second).astype(low)
    far_got = swap(far_total, ACROSS_Z)
    x_fars, g_fars = after((x_fars, g_fars), far_total, dx_near)
    pairs_a = ((x_near, x_fars), (act_a_near, act_a_far)), ((g_near, g_fars), (hid_a_near, hid_a_far))
    sent = jnp.concatenate([weight_sum(r, v, send).astype(low) for r, v in pairs_a], axis=1)
    got = swap(sent, 0)
    kept = [weight_sum(r, v, keep) for r, v in pairs_a]
    first, second = plus(first, near_y[half:]), plus(second, near_x[half:])
    near_first, near_second = swap(first, ACROSS_X), swap(second, ACROSS_Y)
    far_got = after(far_got, from_pair)
    near_total = plane_total(near_own, near_x, near_y, near_first, near_second)
    input_grad = turn((near_total + far_got.astype(wide)).astype(low))
    grads = add_up(*kept, got, after(from_pair, *kept))
    return (input_grad,) + tuple(g[None] for g in grads)


def expert_parts(x_rows, dy_rows, gate_w, up_w, down_w):
    gate_pre = jnp.dot(x_rows, gate_w, preferred_element_type=jnp.float32)
    up_pre = jnp.dot(x_rows, up_w, preferred_element_type=jnp.float32)
    sig_gate = jax.nn.sigmoid(gate_pre)
    active = gate_pre * sig_gate
    hidden = (active * up_pre).astype(jnp.bfloat16)
    hidden_grad = jnp.dot(dy_rows, down_w, preferred_element_type=jnp.float32)
    gate_grad = (hidden_grad * up_pre * sig_gate * (1.0 + gate_pre * (1.0 - sig_gate))).astype(
        jnp.bfloat16
    )
    up_grad = (hidden_grad * active).astype(jnp.bfloat16)
    return (hidden, jnp.concatenate([gate_grad, up_grad], axis=1))


def weight_terms(x_rows, dy_rows, hidden, act_grads):
    first = lax.dot_general(x_rows, act_grads, contract_rows, preferred_element_type=jnp.float32)
    second = lax.dot_general(dy_rows, hidden, contract_rows, preferred_element_type=jnp.float32)
    return jnp.concatenate([first, second], axis=1)


def row_grads(act_grads, both_w):
    return lax.dot_general(
        act_grads, both_w, contract_cols, preferred_element_type=jnp.float32
    ).astype(jnp.bfloat16)


def routed_local(tokens, out_grad, gates, expert_ids, w_gate, w_up, w_down):
    experts = lax.axis_size("expert")
    tok_rows, width = tokens.shape
    top_k = expert_ids.shape[1]
    capacity = 5 * tok_rows * top_k // (4 * experts)
    slot_count = experts * capacity
    flat_ids = expert_ids.reshape(-1)
    expert_match = (flat_ids[:, None] == jnp.arange(experts, dtype=jnp.int32)[None, :]).astype(
        jnp.int32
    )
    earlier = jnp.cumsum(expert_match, axis=0) - expert_match
    position = jnp.sum(earlier * expert_match, axis=1)
    slot_of = flat_ids * capacity + position
    slot_hits = (slot_of[None, :] == jnp.arange(slot_count, dtype=jnp.int32)[:, None]).reshape(
        slot_count, tok_rows, top_k
    )
    pick_tok = jnp.any(slot_hits, axis=2).astype(jnp.bfloat16)
    scale_tok = jnp.sum(jnp.where(slot_hits, gates[None, :, :], jnp.float32(0.0)), axis=2)
    gate_slot = jnp.sum(scale_tok, axis=1)
    send_x = jnp.dot(pick_tok, tokens, preferred_element_type=jnp.float32).astype(jnp.bfloat16)
    send_x = send_x.reshape(experts, capacity, width)
    grad_picked = jnp.dot(pick_tok, out_grad, preferred_element_type=jnp.float32)
    send_dy = (gate_slot[:, None] * grad_picked).astype(jnp.bfloat16)
    send_dy = send_dy.reshape(experts, capacity, width)
    recv_x = lax.all_to_all(send_x, "expert", split_axis=0, concat_axis=0, tiled=True)
    recv_dy = lax.all_to_all(send_dy, "expert", split_axis=0, concat_axis=0, tiled=True)
    full_gate, full_up, full_down = (
        lax.all_gather(w_gate, "dp", axis=1, tiled=True),
        lax.all_gather(w_up, "dp", axis=1, tiled=True),
        lax.all_gather(w_down, "dp", axis=1, tiled=True),
    )
    gate_w = full_gate[0]
    up_w = full_up[0]
    down_w = full_down[0]
    ff_width = gate_w.shape[1]
    both_w = jnp.concatenate([gate_w, up_w], axis=1)
    x_rows = recv_x.reshape(slot_count, width)
    dy_rows = recv_dy.reshape(slot_count, width)
    hidden, act_grads = expert_parts(x_rows, dy_rows, gate_w, up_w, down_w)
    row_out = row_grads(act_grads, both_w)
    returned = lax.all_to_all(
        row_out.reshape(experts, capacity, width), "expert", split_axis=0, concat_axis=0, tiled=True
    )
    grad_sums = lax.psum_scatter(
        weight_terms(x_rows, dy_rows, hidden, act_grads), "dp", scatter_dimension=0, tiled=True
    )
    input_grad = lax.dot_general(
        pick_tok,
        returned.reshape(slot_count, width),
        contract_rows,
        preferred_element_type=jnp.float32,
    ).astype(jnp.bfloat16)
    grad_gate = grad_sums[None, :, :ff_width]
    grad_up = grad_sums[None, :, ff_width : 2 * ff_width]
    grad_down = grad_sums[None, :, 2 * ff_width :]
    return (input_grad, grad_gate, grad_up, grad_down)


def solution(mesh):
    in_specs = (
        P(("expert", "dp"), None),
        P(("expert", "dp"), None),
        P(("expert", "dp"), None),
        P(("expert", "dp"), None),
        P("expert", "dp", None),
        P("expert", "dp", None),
        P("expert", "dp", None),
    )
    out_specs = (
        P(("expert", "dp"), None),
        P("expert", "dp", None),
        P("expert", "dp", None),
        P("expert", "dp", None),
    )
    def local(tokens, *rest):
        tok_rows, experts = tokens.shape[0], mesh.shape["expert"]
        capacity = 5 * tok_rows * rest[1].shape[1] // (4 * experts)
        dense = experts == 16 and mesh.shape["dp"] == 2 and 2 * capacity > tok_rows
        return (dense_local if dense else routed_local)(tokens, *rest)

    return jax.shard_map(
        local, mesh=mesh, in_specs=in_specs, out_specs=out_specs, check_vma=False
    )
```

```python
import jax
import jax.numpy as jnp
from jax import lax
from jax.experimental import pallas as pl
from jax.experimental.pallas import tpu as pltpu
from jax.sharding import PartitionSpec as P

contract_rows = (((0,), (0,)), ((), ()))
contract_cols = (((1,), (1,)), ((), ()))
ACROSS_X, ACROSS_Y, PAIR, ACROSS_Z = 1, 2, 4, 8
low, wide = jnp.bfloat16, jnp.float32


def after(rows, *earlier):
    return lax.optimization_barrier((rows,) + earlier)[0]


def swap(rows, bit):
    if bit == 0:
        return lax.ppermute(rows, "dp", [(0, 1), (1, 0)])
    experts = lax.axis_size("expert")
    return lax.ppermute(rows, "expert", [(i, i ^ bit) for i in range(experts)])


def swap_far(rows, bit):
    experts = lax.axis_size("expert")
    groups = [[i, i ^ bit] for i in range(experts) if i < i ^ bit]
    both = lax.all_to_all(
        jnp.stack([rows, rows]), "expert", split_axis=0, concat_axis=0, tiled=True, axis_index_groups=groups
    )
    return jnp.where(lax.axis_index("expert") & bit == 0, both[1], both[0])


def turn(rows):
    half = rows.shape[1] // 2
    turned = jnp.concatenate([rows[:, half:], rows[:, :half]], axis=1)
    return jnp.where(lax.axis_index("dp") == 0, rows, turned)


def gate_rows(gates, expert_ids, experts):
    count = gates.shape[0]
    lanes = lax.broadcasted_iota(jnp.int32, (1, experts * count), 1) // count
    ids = jnp.tile(expert_ids.T, (1, experts))
    spread = jnp.sum(jnp.where(ids == lanes, jnp.tile(gates.T, (1, experts)), 0.0), axis=0, keepdims=True)
    first = lax.reduce_precision(spread, 8, 7)
    second = lax.reduce_precision(spread - first, 8, 7)
    third = spread - first - second
    empty = jnp.zeros((5, experts * count), wide)
    return jnp.concatenate([first, second, third, empty], axis=0).astype(low)


def scale_of(block, rows, expert):
    terms = lax.dynamic_slice(block, (rows, expert * rows), (8, rows))
    return jnp.sum(terms.astype(wide), axis=0)


def activations(pre, out_pre, scale):
    ff = out_pre.shape[1]
    gate_pre, up_pre = pre[:, :ff], pre[:, ff:]
    hidden_grad = scale * out_pre
    sig_gate = jax.nn.sigmoid(gate_pre)
    active = gate_pre * sig_gate
    hidden = (scale * (active * up_pre)).astype(low)
    gate_grad = (hidden_grad * up_pre * sig_gate * (1.0 + gate_pre * (1.0 - sig_gate))).astype(low)
    up_grad = (hidden_grad * active).astype(low)
    return hidden, jnp.concatenate([gate_grad, up_grad], axis=1)


def dot(a, b, dims=(((1,), (0,)), ((), ()))):
    return lax.dot_general(a, b, dims, preferred_element_type=wide)


def plane_sends(dx):
    quarter = dx.shape[0] // 4
    half = quarter // 2
    own, of_x, of_y, of_xy = [dx[i * quarter : (i + 1) * quarter] for i in range(4)]
    to_y = jnp.concatenate([of_y[:half], of_xy[:half]], axis=0)
    to_x = jnp.concatenate([of_x[half:], of_xy[half:]], axis=0)
    return to_x, to_y, of_x[:half], of_y[half:], own


def plus(a, b):
    return (a.astype(wide) + b.astype(wide)).astype(low)


def plane_total(own, got_x, got_y, got_first, got_second):
    half = got_first.shape[0]
    got = (
        jnp.concatenate([got_y[:half], got_x[:half]], axis=0).astype(wide)
        + jnp.concatenate([got_first, got_second], axis=0).astype(wide)
    )
    return own.astype(wide) + got


def dx_kernel(act_a, act_b, w_a, w_b, out):
    out[...] = (dot(act_a[...], w_a[...], contract_cols) + dot(act_b[...], w_b[...], contract_cols)).astype(low)


def dx_rows(act_a, act_b, w_a, w_b):
    rows, depth = act_a.shape
    width = w_a.shape[0]
    tile = min(width, 512)
    whole = pl.BlockSpec((rows, depth), lambda i: (0, 0))
    part = pl.BlockSpec((tile, depth), lambda i: (i, 0))
    return pl.pallas_call(
        dx_kernel,
        grid=(width // tile,),
        in_specs=[whole, whole, part, part],
        out_specs=pl.BlockSpec((rows, tile), lambda i: (0, i)),
        out_shape=jax.ShapeDtypeStruct((rows, width), low),
        compiler_params=pltpu.CompilerParams(vmem_limit_bytes=16 << 20),
        cost_estimate=pl.CostEstimate(
            flops=4 * rows * depth * width, bytes_accessed=4 * width * depth + 2 * rows * width, transcendentals=0
        ),
    )(act_a, act_b, w_a, w_b)


def add_up(kept_both, kept_down, got, more):
    rows, ff = kept_down.shape
    tile = min(rows, 256)

    def kernel(both, down, got, more, gate_out, up_out, down_out):
        extra = got[...].astype(wide) + more[...].astype(wide)
        gate_out[...] = both[:, :ff] + extra[:, :ff]
        up_out[...] = both[:, ff:] + extra[:, ff : 2 * ff]
        down_out[...] = down[...] + extra[:, 2 * ff :]

    def part(columns):
        return pl.BlockSpec((tile, columns), lambda i: (i, 0))

    return pl.pallas_call(
        kernel,
        grid=(rows // tile,),
        in_specs=[part(2 * ff), part(ff), part(3 * ff), part(3 * ff)],
        out_specs=[part(ff)] * 3,
        out_shape=[jax.ShapeDtypeStruct((rows, ff), wide)] * 3,
        compiler_params=pltpu.CompilerParams(vmem_limit_bytes=16 << 20),
        cost_estimate=pl.CostEstimate(flops=20_000_000_000, bytes_accessed=0, transcendentals=0),
    )(kept_both, kept_down, got, more)


def dense_local(tokens, out_grad, gates, expert_ids, w_gate, w_up, w_down):
    experts = lax.axis_size("expert")
    tok_rows, width = tokens.shape
    mid = width // 2
    ff = w_gate.shape[2]
    me = lax.axis_index("expert")
    pair = me ^ PAIR

    def join(parts):
        return jnp.concatenate([p[:tok_rows] for p in parts], axis=0)

    def scales(parts, expert):
        return jnp.concatenate([scale_of(p, tok_rows, expert) for p in parts])[:, None]

    def weight_sum(rows, acts, columns):
        return sum(dot(r[:, columns], a, contract_rows) for r, a in zip(rows, acts))

    keep, send = slice(0, mid), slice(mid, width)

    gate_mine, up_mine, down_mine = w_gate[0], w_up[0], w_down[0]
    both_mine = jnp.concatenate([gate_mine, up_mine], axis=1)
    x_own = turn(tokens)
    g_own = jnp.concatenate([turn(out_grad), gate_rows(gates, expert_ids, experts)], axis=0)
    x_x = swap(x_own, ACROSS_X)
    g_y = swap(g_own, ACROSS_Y)
    gate_pair, up_pair = swap(gate_mine, PAIR), swap(up_mine, PAIR)
    both_pair = jnp.concatenate([gate_pair, up_pair], axis=1)
    far = swap_far(jnp.concatenate([x_own, g_own], axis=0), ACROSS_Z)
    g_x = swap(after(g_own, x_x, g_y), ACROSS_X)
    x_y = swap(after(x_own, x_x, g_y), ACROSS_Y)
    g_y, x_x = after((g_y, x_x), g_x, x_y)
    g_xy = swap(g_y, ACROSS_X)
    x_xy = swap(x_x, ACROSS_Y)
    far = after(far, g_xy, x_xy)
    far_of_x = swap(far, ACROSS_X)
    far_of_y = swap(far, ACROSS_Y)
    x_near_parts = x_own, x_x, x_y, x_xy
    g_near_parts = g_own, g_x, g_y, after(g_xy, both_pair)
    x_near, g_near = join(x_near_parts), join(g_near_parts)
    x_near, g_near = lax.optimization_barrier((x_near, g_near))
    scale_a_near, scale_b_near = scales(g_near_parts, me), scales(g_near_parts, pair)
    down_pair = swap(after(down_mine, far), PAIR)
    far_of_x, far_of_y = after((far_of_x, far_of_y), x_near, g_near)
    g_far_xy = swap(far_of_y[tok_rows:], ACROSS_X)
    x_far_xy = swap(far_of_x[:tok_rows], ACROSS_Y)
    both_pair = after(both_pair, far_of_x, far_of_y)
    both_pair_other = swap(both_pair, 0)
    both_b = jnp.concatenate([both_pair, both_pair_other], axis=0)
    pre_b_near = dot(x_near, both_b)
    down_pair = after(down_pair, x_far_xy)
    down_pair_other = swap(down_pair, 0)
    down_b = jnp.concatenate([down_pair, down_pair_other], axis=0)
    x_far, x_far_x, x_far_y = [v[:tok_rows] for v in (far, far_of_x, far_of_y)]
    g_far, g_far_x, g_far_y = [v[tok_rows:] for v in (far, far_of_x, far_of_y)]
    hid_b_near, act_b_near = activations(pre_b_near, dot(g_near, down_b), scale_b_near)
    x_far, x_far_x, x_far_y = [v[:tok_rows] for v in (far, far_of_x, far_of_y)]
    g_far, g_far_x, g_far_y = [v[tok_rows:] for v in (far, far_of_x, far_of_y)]
    x_far_parts = (x_far, x_far_x, x_far_y, x_far_xy)
    g_far_parts = (g_far, g_far_x, g_far_y, g_far_xy)
    x_fars, g_fars = lax.optimization_barrier((join(x_far_parts), join(g_far_parts)))
    hid_b_far, act_b_far = activations(
        dot(x_fars, both_b), dot(g_fars, down_b), scales(g_far_parts, pair)
    )
    pairs_b = ((x_near, x_fars), (act_b_near, act_b_far)), ((g_near, g_fars), (hid_b_near, hid_b_far))
    sent = jnp.concatenate([weight_sum(r, v, send).astype(low) for r, v in pairs_b], axis=1)
    got = swap(sent, 0)
    kept = [weight_sum(r, v, keep) for r, v in pairs_b]
    for_pair = (jnp.concatenate(kept, axis=1) + got.astype(wide)).astype(low)
    from_pair = swap(for_pair, PAIR)
    both_other = swap(after(both_mine, for_pair), 0)
    down_other = swap(after(down_mine, for_pair), 0)
    both_a = jnp.concatenate([both_mine, both_other], axis=0)
    down_a = jnp.concatenate([down_mine, down_other], axis=0)
    x_fars, g_fars, x_near, g_near, both_a, down_a = after(
        (x_fars, g_fars, x_near, g_near, both_a, down_a), for_pair
    )
    hid_a_far, act_a_far = activations(
        dot(x_fars, both_a), dot(g_fars, down_a), scales(g_far_parts, me)
    )
    to_x, to_y, first, second, far_own = plane_sends(dx_rows(act_a_far, act_b_far, both_a, both_b))
    far_x, far_y = swap(to_x, ACROSS_X), swap(to_y, ACROSS_Y)
    x_near, g_near = after((x_near, g_near), to_x, to_y)
    hid_a_near, act_a_near = activations(dot(x_near, both_a), dot(g_near, down_a), scale_a_near)
    half = tok_rows // 2
    dx_near = dx_rows(act_a_near, act_b_near, both_a, both_b)
    first, second = plus(first, far_y[half:]), plus(second, far_x[half:])
    far_first, far_second = swap(first, ACROSS_X), swap(second, ACROSS_Y)
    dx_near = after(dx_near, first, second)
    to_x, to_y, first, second, near_own = plane_sends(dx_near)
    near_x, near_y = swap(to_x, ACROSS_X), swap(to_y, ACROSS_Y)
    far_total = plane_total(far_own, far_x, far_y, far_first, far_second).astype(low)
    far_got = swap(far_total, ACROSS_Z)
    x_fars, g_fars = after((x_fars, g_fars), far_total, dx_near)
    pairs_a = ((x_near, x_fars), (act_a_near, act_a_far)), ((g_near, g_fars), (hid_a_near, hid_a_far))
    sent = jnp.concatenate([weight_sum(r, v, send).astype(low) for r, v in pairs_a], axis=1)
    got = swap(sent, 0)
    kept = [weight_sum(r, v, keep) for r, v in pairs_a]
    first, second = plus(first, near_y[half:]), plus(second, near_x[half:])
    near_first, near_second = swap(first, ACROSS_X), swap(second, ACROSS_Y)
    far_got = after(far_got, from_pair)
    near_total = plane_total(near_own, near_x, near_y, near_first, near_second)
    input_grad = turn((near_total + far_got.astype(wide)).astype(low))
    grads = add_up(*kept, got, after(from_pair, *kept))
    return (input_grad,) + tuple(g[None] for g in grads)


def expert_parts(x_rows, dy_rows, gate_w, up_w, down_w):
    gate_pre = jnp.dot(x_rows, gate_w, preferred_element_type=jnp.float32)
    up_pre = jnp.dot(x_rows, up_w, preferred_element_type=jnp.float32)
    sig_gate = jax.nn.sigmoid(gate_pre)
    active = gate_pre * sig_gate
    hidden = (active * up_pre).astype(jnp.bfloat16)
    hidden_grad = jnp.dot(dy_rows, down_w, preferred_element_type=jnp.float32)
    gate_grad = (hidden_grad * up_pre * sig_gate * (1.0 + gate_pre * (1.0 - sig_gate))).astype(
        jnp.bfloat16
    )
    up_grad = (hidden_grad * active).astype(jnp.bfloat16)
    return (hidden, jnp.concatenate([gate_grad, up_grad], axis=1))


def weight_terms(x_rows, dy_rows, hidden, act_grads):
    first = lax.dot_general(x_rows, act_grads, contract_rows, preferred_element_type=jnp.float32)
    second = lax.dot_general(dy_rows, hidden, contract_rows, preferred_element_type=jnp.float32)
    return jnp.concatenate([first, second], axis=1)


def row_grads(act_grads, both_w):
    return lax.dot_general(
        act_grads, both_w, contract_cols, preferred_element_type=jnp.float32
    ).astype(jnp.bfloat16)


def routed_local(tokens, out_grad, gates, expert_ids, w_gate, w_up, w_down):
    experts = lax.axis_size("expert")
    tok_rows, width = tokens.shape
    top_k = expert_ids.shape[1]
    capacity = 5 * tok_rows * top_k // (4 * experts)
    slot_count = experts * capacity
    flat_ids = expert_ids.reshape(-1)
    expert_match = (flat_ids[:, None] == jnp.arange(experts, dtype=jnp.int32)[None, :]).astype(
        jnp.int32
    )
    earlier = jnp.cumsum(expert_match, axis=0) - expert_match
    position = jnp.sum(earlier * expert_match, axis=1)
    slot_of = flat_ids * capacity + position
    slot_hits = (slot_of[None, :] == jnp.arange(slot_count, dtype=jnp.int32)[:, None]).reshape(
        slot_count, tok_rows, top_k
    )
    pick_tok = jnp.any(slot_hits, axis=2).astype(jnp.bfloat16)
    scale_tok = jnp.sum(jnp.where(slot_hits, gates[None, :, :], jnp.float32(0.0)), axis=2)
    gate_slot = jnp.sum(scale_tok, axis=1)
    send_x = jnp.dot(pick_tok, tokens, preferred_element_type=jnp.float32).astype(jnp.bfloat16)
    send_x = send_x.reshape(experts, capacity, width)
    grad_picked = jnp.dot(pick_tok, out_grad, preferred_element_type=jnp.float32)
    send_dy = (gate_slot[:, None] * grad_picked).astype(jnp.bfloat16)
    send_dy = send_dy.reshape(experts, capacity, width)
    recv_x = lax.all_to_all(send_x, "expert", split_axis=0, concat_axis=0, tiled=True)
    recv_dy = lax.all_to_all(send_dy, "expert", split_axis=0, concat_axis=0, tiled=True)
    full_gate, full_up, full_down = (
        lax.all_gather(w_gate, "dp", axis=1, tiled=True),
        lax.all_gather(w_up, "dp", axis=1, tiled=True),
        lax.all_gather(w_down, "dp", axis=1, tiled=True),
    )
    gate_w = full_gate[0]
    up_w = full_up[0]
    down_w = full_down[0]
    ff_width = gate_w.shape[1]
    both_w = jnp.concatenate([gate_w, up_w], axis=1)
    x_rows = recv_x.reshape(slot_count, width)
    dy_rows = recv_dy.reshape(slot_count, width)
    hidden, act_grads = expert_parts(x_rows, dy_rows, gate_w, up_w, down_w)
    row_out = row_grads(act_grads, both_w)
    returned = lax.all_to_all(
        row_out.reshape(experts, capacity, width), "expert", split_axis=0, concat_axis=0, tiled=True
    )
    grad_sums = lax.psum_scatter(
        weight_terms(x_rows, dy_rows, hidden, act_grads), "dp", scatter_dimension=0, tiled=True
    )
    input_grad = lax.dot_general(
        pick_tok,
        returned.reshape(slot_count, width),
        contract_rows,
        preferred_element_type=jnp.float32,
    ).astype(jnp.bfloat16)
    grad_gate = grad_sums[None, :, :ff_width]
    grad_up = grad_sums[None, :, ff_width : 2 * ff_width]
    grad_down = grad_sums[None, :, 2 * ff_width :]
    return (input_grad, grad_gate, grad_up, grad_down)


def solution(mesh):
    in_specs = (
        P(("expert", "dp"), None),
        P(("expert", "dp"), None),
        P(("expert", "dp"), None),
        P(("expert", "dp"), None),
        P("expert", "dp", None),
        P("expert", "dp", None),
        P("expert", "dp", None),
    )
    out_specs = (
        P(("expert", "dp"), None),
        P("expert", "dp", None),
        P("expert", "dp", None),
        P("expert", "dp", None),
    )
    def local(tokens, *rest):
        tok_rows, experts = tokens.shape[0], mesh.shape["expert"]
        capacity = 5 * tok_rows * rest[1].shape[1] // (4 * experts)
        dense = experts == 16 and mesh.shape["dp"] == 2 and 2 * capacity > tok_rows
        return (dense_local if dense else routed_local)(tokens, *rest)

    return jax.shard_map(
        local, mesh=mesh, in_specs=in_specs, out_specs=out_specs, check_vma=False
    )
```
